128 devices in a mesh: blk: 32 (over z, y_hi, x), rep: 4 (over y_lo, core).
Axes of the slice: x: 4, y: 4 (y_hi: 2, y_lo: 2; y = y_hi * 2 + y_lo), z: 4, core: 2. Of those that a mesh axis runs over, the one named last changes fastest.
Arguments:
- features: bfloat16 [16384, 128], P(('blk', 'rep'))
- owner_row: int32 [16384], P(('blk', 'rep')), may hold values from 0 to 16383, as said below
- value_probe: bfloat16 [8, 16384], P(None, 'blk'), may hold values from -6 to 6
- grad_probe: bfloat16 [16384, 1024], P('blk'), may hold values from -6 to 6
Outputs:
- value_out: float32 [8, 16384], P(None, ('blk', 'rep'))
- grad_out: float32 [16384, 1024], P(('blk', 'rep'))
The draws below stay inside these ranges and needn't reach their ends.
Inputs may be any that keep to these rules, and one draw needn't show every extreme that they name: `owner_row`: A permutation. The data shard of device (a, r), rows (a 4 + r) * 128 to (a 4 + r + 1) * 128 - 1 with blk index a and rep index r, sends exactly 4 rows to every row block b, all into that block's rows b * 512 + r * 128 to b * 512 + (r + 1) * 128 - 1.
All inputs are finite; a program needn't handle non-finite values.
Results may differ from the reference program's by a relative error of at most 0.002.
Values may be sent and summed in bfloat16 or wider, within the bound.
A program may use at most 64 MiB of HBM per device.

```python
import jax
import jax.numpy as jnp
from jax import lax

BLOCK = 512
D = 128
PROBES = 8
POINTS = 16384
QUARTER = 128
N_BLK = 32
N_REP = 4


def draw_features(key, part):
    key = jax.random.fold_in(key, 11)
    return jax.random.normal(key, (POINTS, D), jnp.float32).astype(jnp.bfloat16)


def draw_owner_row(key, part):
    key = jax.random.fold_in(key, 23)
    group_rows = QUARTER // N_BLK
    source_keys = jax.random.split(jax.random.fold_in(key, 1), N_REP * N_BLK)
    target_keys = jax.random.split(jax.random.fold_in(key, 2), N_REP * N_BLK)
    sigma = jax.vmap(lambda k: jax.random.permutation(k, QUARTER))(source_keys)
    tau = jax.vmap(lambda k: jax.random.permutation(k, QUARTER))(target_keys)
    rep_idx = jnp.arange(N_REP, dtype=jnp.int32)[:, None, None]
    block_idx = jnp.arange(N_BLK, dtype=jnp.int32)[None, :, None]
    slot_idx = jnp.arange(QUARTER, dtype=jnp.int32)[None, None, :]
    source = (slot_idx // group_rows + block_idx) % N_BLK
    local = block_idx * group_rows + slot_idx % group_rows
    owner = block_idx * BLOCK + rep_idx * QUARTER + tau[rep_idx * N_BLK + block_idx, slot_idx]
    data_row = (source * N_REP + rep_idx) * QUARTER + sigma[rep_idx * N_BLK + source, local]
    shape = (N_REP, N_BLK, QUARTER)
    owner = jnp.broadcast_to(owner, shape).reshape(-1).astype(jnp.int32)
    data_row = jnp.broadcast_to(data_row, shape).reshape(-1).astype(jnp.int32)
    return jnp.zeros((POINTS,), jnp.int32).at[data_row].set(owner)


def shard_levels(key, extent, cuts, low, high):
    def one(dim, shards_of):
        heights = jax.random.uniform(jax.random.fold_in(jax.random.fold_in(key, 6), dim), (shards_of,), jnp.float32, low / len(cuts), high / len(cuts))
        return jnp.repeat(jnp.exp(heights), extent[dim] // shards_of).reshape((-1,) + (1,) * (len(extent) - dim - 1))

    gain = one(*cuts[0])
    for cut in cuts[1:]:
        gain = gain * one(*cut)
    return gain


def gaussian(key, extent, scale, reach, shards=(), kind=jnp.bfloat16):
    array = jax.random.normal(key, extent, jnp.float32) * scale
    if len(shards) > 0:
        array = shard_levels(key, extent, shards, -0.22, 0.18) * array
    return jnp.clip(array, min=-reach, max=reach).astype(kind)


def setup_inputs(seed: int = 0) -> dict:
    keys = jax.random.split(jax.random.key(seed), 5)
    return {
        "features": draw_features(jax.random.fold_in(keys[4], 71), 0),
        "owner_row": draw_owner_row(jax.random.fold_in(keys[4], 71), 0),
        "value_probe": gaussian(keys[2], (PROBES, POINTS), 1.0, 6.0, ((1, 32),)),
        "grad_probe": gaussian(keys[3], (POINTS, PROBES * D), 1.0, 6.0, ((0, 32),)),
    }


def pair_terms(own_rows, column, scaling, totals):
    col_rows, col_values, col_grads = column
    values, grads = totals
    square = scaling * scaling
    own_wide = own_rows.astype(jnp.float32)
    col_wide = col_rows.astype(jnp.float32)
    own_norm = jnp.sum(own_wide * own_wide, 1)
    col_norm = jnp.sum(col_wide * col_wide, 1)
    gram = jnp.dot(own_rows, col_rows.T, preferred_element_type=jnp.float32)
    kernel = jnp.exp(-0.5 * (square * own_norm[:, None] + square * col_norm[None, :] - 2.0 * square * gram))
    shaped = col_grads.astype(jnp.float32).reshape(col_rows.shape[0], PROBES, D)
    anchor = jnp.einsum("jd,jpd->pj", col_wide, shaped) * scaling
    inner = jnp.einsum("id,jpd->ipj", own_wide, shaped) * scaling - anchor[None]
    coef = kernel[:, None, :] * (col_values.astype(jnp.float32)[None] + inner)
    sums = jnp.sum(coef, 2)
    coef_low = lax.optimization_barrier(coef.astype(jnp.bfloat16)).astype(jnp.float32)
    cross = jnp.einsum("ipj,jd->ipd", coef_low, col_wide).reshape(own_rows.shape[0], PROBES * D) * scaling
    spread = jnp.dot(kernel.astype(jnp.bfloat16), col_grads, preferred_element_type=jnp.float32)
    pull = ((own_wide * scaling)[:, None, :] * sums[:, :, None]).reshape(own_rows.shape[0], PROBES * D)
    return values + sums, grads + spread + cross - pull


def reference(features, owner_row, value_probe, grad_probe):
    scaling = (4.0 * D) ** -0.25
    owned = jnp.zeros((POINTS, D), jnp.bfloat16).at[owner_row].set(features)
    row_blocks = owned.reshape(N_BLK, BLOCK, D)
    value_blocks = value_probe.reshape(PROBES, N_BLK, BLOCK).transpose(1, 0, 2)
    grad_blocks = grad_probe.reshape(N_BLK, BLOCK, PROBES * D)

    def one_block(own_rows):
        def advance(totals, column):
            return pair_terms(own_rows, column, scaling, totals), None

        start = (jnp.zeros((BLOCK, PROBES), jnp.float32), jnp.zeros((BLOCK, PROBES * D), jnp.float32))
        totals, unused = lax.scan(advance, start, (row_blocks, value_blocks, grad_blocks))
        return totals

    values, grads = lax.map(one_block, row_blocks)
    return values.reshape(POINTS, PROBES).T, grads.reshape(POINTS, PROBES * D)
```

```python
import functools

import jax
import jax.numpy as jnp
from jax import lax
from jax.experimental import pallas as pl
from jax.experimental.pallas import tpu as pltpu
from jax.sharding import PartitionSpec as P

F32, BF16 = jnp.float32, jnp.bfloat16
MESH = pl.DeviceIdType.MESH
LOG2E = 1.4426950408889634
WIRE = BF16

SLOTS = (
    (0, 0), (1, 0), (3, 0), (0, 1),
    (0, 3), (2, 0), (0, 2), (1, 1),
    (1, 3), (3, 1), (3, 3), (2, 1), (2, 3), (1, 2), (3, 2), (2, 2),
)
NEAR = ((1, 0), (3, 0), (0, 1), (0, 3))
SECOND = ((2, 0), (1, 1), (3, 3), (1, 3), (3, 1), (0, 2))
THIRD = ((2, 1), (2, 3), (1, 2), (3, 2))
LAST = ((2, 2),)


def nt(a, b):
    return lax.dot_general(a, b, (((1,), (1,)), ((), ())), preferred_element_type=F32)


def nn(a, b):
    return jnp.dot(a, b, preferred_element_type=F32)


def split3(a):
    hi = a.astype(BF16)
    rest = a - hi.astype(F32)
    mid = rest.astype(BF16)
    return hi, mid, (rest - mid.astype(F32)).astype(BF16)


def kernel(
    feat, row_r, row_c, vprobe, gprobe, vout, gout,
    M, N, G, Z, W, OWN, BI, X, V, KB, KS, DB, PB, VIA, RX, VS, VR,
    a2a_s, a2a_r, own_s, own_r, loc, g_s, g_r, z_s, z_r, d_s, d_r, y_s, via_r, rx_r, v_s, v_r,
):
    rho = 512.0 ** -0.25
    c1 = rho * rho * LOG2E
    b, r = lax.axis_index("blk"), lax.axis_index("rep")
    x, z = b % 4, b // 8
    y, core = (b // 4) % 2 * 2 + r // 2, r % 2

    def at_xz(dx, dz):
        return ((z + dz) % 4 * 8 + b // 4 % 2 * 4 + (x + dx) % 4, r)

    def at_y(dy, dc):
        yy = (y + dy) % 4
        return (z * 8 + yy // 2 * 4 + x, yy % 2 * 2 + (core + dc) % 2)

    def remote(src, dst, ss, rs, dev):
        return pltpu.make_async_remote_copy(
            src_ref=src, dst_ref=dst, send_sem=ss, recv_sem=rs, device_id=dev, device_id_type=MESH)

    mine = pltpu.make_async_copy(gprobe.at[pl.ds(pl.multiple_of(r * 128, 128), 128), :], G.at[0], loc)
    mine.start()

    oc, orow = row_c[...], row_r[...]
    rank = jnp.sum((oc < orow).astype(F32), axis=0, keepdims=True)
    q = lax.broadcasted_iota(jnp.int32, (256, 128), 0)
    pick = (rank == (q // 8 * 4 + q % 4).astype(F32)).astype(BF16)
    slot = jnp.broadcast_to((oc % 128).astype(F32), (128, 128)).astype(BF16)
    both = nn(pick, jnp.concatenate([feat[...], slot], axis=1))
    M[...] = jnp.where(q % 8 < 4, both[:, :128], both[:, 128:]).reshape(32, 8, 128)

    barrier = pltpu.get_barrier_semaphore()

    def greet(k, _):
        pl.semaphore_signal(barrier, inc=1, device_id=((b + k) % 32, r), device_id_type=MESH)
        return 0

    lax.fori_loop(1, 32, greet, 0)
    for dy, dc in ((1, 0), (3, 0), (0, 1), (1, 1), (2, 1), (3, 1)):
        pl.semaphore_signal(barrier, inc=1, device_id=at_y(dy, dc), device_id_type=MESH)
    pl.semaphore_wait(barrier, 37)

    def deal(k, _):
        to = (b + k) % 32
        remote(M.at[to], N.at[k], a2a_s, a2a_r, (to, r)).start()
        return 0

    lax.fori_loop(1, 32, deal, 0)
    N[0] = M[b]

    chans = {"g": (G, 64, g_s, g_r), "z": (Z, 80, z_s, z_r)}

    def piece(ch, h, s):
        buf, rows, ss, rs = chans[ch]
        return buf.at[s, pl.ds(h * rows, rows), :]

    def slot_of(h, i1, i2):
        return SLOTS.index((i1 % 4, i2 % 4) if h == 0 else (i2 % 4, i1 % 4))

    def send(ch, h, i1, i2, e1, e2):
        buf, rows, ss, rs = chans[ch]
        t = slot_of(h, i1 + e1, i2 + e2)
        remote(piece(ch, h, slot_of(h, i1, i2)), piece(ch, h, t), ss, rs.at[h, t],
               at_xz(e1, e2) if h == 0 else at_xz(e2, e1)).start()

    def handle(ch, h, i1, i2):
        buf, rows, ss, rs = chans[ch]
        if (i1, i2) != (0, 0):
            s = slot_of(h, i1, i2)
            remote(piece(ch, h, s), piece(ch, h, s), ss, rs.at[h, s], (b, r)).wait_recv()
        if i2 == 0:
            if i1 == 0 or (i1 == 1 and h == 0):
                send(ch, h, i1, 0, 1, 0)
            if i1 == 0 or (i1 == 3 and h == 1):
                send(ch, h, i1, 0, -1, 0)
            send(ch, h, i1, 0, 0, 1)
            send(ch, h, i1, 0, 0, -1)
        if i2 == 1 and i1 in (0, 1):
            send(ch, h, i1, 1, 0, 1)
        if i2 == 3 and i1 in (3, 2):
            send(ch, h, i1, 3, 0, -1)

    def events(ch, items):
        for i1, i2 in items:
            for h in (0, 1):
                handle(ch, h, i1, i2)

    mine.wait()
    events("g", ((0, 0),))

    X[...] = jnp.zeros_like(X)
    V[...] = jnp.zeros_like(V)

    remote(M.at[pl.ds(0, 31)], N.at[pl.ds(1, 31)], a2a_s, a2a_r, (b, r)).wait_recv()
    n2 = N[...].reshape(256, 128)
    marks = n2.T[0:1, :]
    lane = lax.broadcasted_iota(jnp.int32, (128, 256), 1)
    want = lax.broadcasted_iota(jnp.int32, (128, 256), 0).astype(F32)
    put = ((marks == want) & (lane % 8 >= 4)).astype(BF16)
    placed32 = nn(put, pltpu.roll(n2, 4, 0).astype(BF16))
    placed = placed32.astype(BF16)
    Z[0, 0:128, :] = placed
    OWN[896:1024, :] = placed
    for k, dy in enumerate((2, 1, 3, 0)):
        for dc in (1, 0):
            if (dy, dc) != (0, 0):
                at = (2, 1, 3, 0).index((-dy) % 4) * 256 + (0 if dc else 128)
                remote(OWN.at[pl.ds(896, 128), :], OWN.at[pl.ds(at, 128), :], own_s, own_r, at_y(dy, dc)).start()

    rows = []
    for p in range(8):
        rows.append(jnp.sum((placed32 * G[0, :, p * 128:(p + 1) * 128].astype(F32)).T, axis=0, keepdims=True))
    anchor = jnp.concatenate(rows, axis=0)
    vp = vprobe[:, pl.ds(pl.multiple_of(r * 128, 128), 128)].astype(F32)
    w = vp * (1.0 / rho) - anchor
    norm = (0.5 * c1) * jnp.sum((placed32 * placed32).T, axis=0, keepdims=True)
    eight = lax.broadcasted_iota(jnp.int32, (8, 128), 0)
    n_hi, n_mid, n_lo = split3(jnp.broadcast_to(norm, (8, 128)))
    tail = jnp.where(eight == 0, n_hi.astype(F32), jnp.where(
        eight == 1, n_mid.astype(F32), jnp.where(eight == 2, n_lo.astype(F32), 0.0)))
    Z[0, 128:160, :] = jnp.concatenate([part.astype(F32) for part in split3(w)] + [tail], axis=0).astype(BF16)
    events("z", ((0, 0),))

    def unpack(s0, count):
        for s in range(s0, s0 + count):
            aux = Z[s, 128:160, :].astype(F32)
            W[s, 0:8, :] = aux[0:8] + aux[8:16] + aux[16:24]
            W[s, 8:9, :] = aux[24:25] + aux[25:26] + aux[26:27]

    events("g", NEAR)
    remote(OWN.at[pl.ds(0, 896), :], OWN.at[pl.ds(0, 896), :], own_s, own_r, (b, r)).wait_recv()
    wide = OWN[...].astype(F32)
    BI[...] = (0.5 * c1) * jnp.sum(wide * wide, axis=1, keepdims=True)
    events("z", NEAR)
    unpack(0, 4)

    def tile(ii, s0, ns, TI):
        TJ = ns * 128
        zz = Z[pl.ds(s0, ns), 0:128, :].reshape(TJ, 128)
        own = OWN[ii, :]
        bj = jnp.concatenate([W[s0 + q, 8:9, :] for q in range(ns)], axis=1)
        k = jnp.exp2(nt(own, zz) * c1 - BI[ii, :] - bj)
        kbig, klow = (KS[0], KB[0]) if ns == 4 else (KS[1], KB[1])
        kbig[...] = k * rho
        klow[...] = k.astype(BF16)
        for hh in range(4):
            hs = pl.ds(hh * 256, 256)
            X[ii, hs] += nn(klow[...], G[pl.ds(s0, ns), :, hs].reshape(TJ, 256))
            for p in (2 * hh, 2 * hh + 1):
                ps = pl.ds(p * 128, 128)
                inner = nt(own, G[pl.ds(s0, ns), :, ps].reshape(TJ, 128))
                wr = jnp.concatenate([W[s0 + q, p:p + 1, :] for q in range(ns)], axis=1)
                coef = kbig[...] * (inner + wr)
                part = coef[:, 0:128]
                for q in range(1, ns):
                    part = part + coef[:, q * 128:(q + 1) * 128]
                V[p, ii, :] += part
                X[ii, ps] += nn(coef.astype(BF16), zz) * rho

    def early(n, _):
        @pl.when(n == 2)
        def _():
            for ch in ("g", "z"):
                events(ch, SECOND)
            unpack(4, 4)

        @pl.when(n == 3)
        def _():
            for ch in ("g", "z"):
                events(ch, THIRD)

        tile(pl.ds(pl.multiple_of(n % 2 * 512, 512), 512), n // 2 * 4, 4, 512)
        return 0

    lax.fori_loop(0, 4, early, 0)
    for ch in ("g", "z"):
        events(ch, LAST)
    unpack(8, 8)

    def core_swap(k):
        return remote(X.at[pl.ds(pl.multiple_of(k * 256, 256), 128), :], DB.at[k], d_s.at[k], d_r.at[k], at_y(0, 1))

    def merged(k):
        core_swap(k).wait_recv()
        return X[k * 256 + 128:k * 256 + 256, :] + DB[k]

    def via(j):
        half = pl.ds(64 * j, 64)
        return remote(PB.at[0, half, :], VIA.at[j], y_s.at[j], via_r.at[j], at_y(1 - 2 * j, 0))

    def step_y(j):
        return remote(PB.at[1 + j], RX.at[j], y_s.at[2 + j], rx_r.at[j], at_y(1 - 2 * j, 0))

    def late(k, _):
        at = pl.multiple_of(k * 256, 256)
        ii = pl.ds(at, 256)
        tile(ii, 8, 8, 256)
        own = OWN[ii, :].astype(F32) * rho
        lanes = lax.broadcasted_iota(jnp.int32, (256, 128), 1)
        vt = jnp.zeros((256, 128), F32)
        for p in range(8):
            col = jnp.sum(V[p, ii, :], axis=1, keepdims=True)
            X[ii, pl.ds(p * 128, 128)] -= own * col
            vt = jnp.where(lanes == p, col, vt)
        core_swap(k).start()
        dy = (2 + 3 * (k % 2) + (k // 2) * (1 + 2 * (k % 2))) % 4
        VS[2 * k] = vt[0:128].T[0:8]
        VS[2 * k + 1] = vt[128:256].T[0:8]
        remote(VS.at[2 * k], VR.at[2 * k], v_s, v_r, at_y(dy, 1)).start()

        @pl.when(k < 3)
        def _():
            remote(VS.at[2 * k + 1], VR.at[2 * k + 1], v_s, v_r, at_y(dy, 0)).start()

        @pl.when(k == 1)
        def _():
            PB[0] = merged(0).astype(WIRE)
            via(0).start()
            via(1).start()

        @pl.when(k == 2)
        def _():
            via(0).wait_recv()
            whole = merged(1)
            PB[1, 0:64, :] = (whole[0:64] + VIA[0].astype(F32)).astype(WIRE)
            PB[1, 64:128, :] = whole[64:128].astype(WIRE)
            step_y(0).start()

        @pl.when(k == 3)
        def _():
            via(1).wait_recv()
            whole = merged(2)
            PB[2, 0:64, :] = whole[0:64].astype(WIRE)
            PB[2, 64:128, :] = (whole[64:128] + VIA[1].astype(F32)).astype(WIRE)
            step_y(1).start()

        return 0

    lax.fori_loop(0, 4, late, 0)
    total = merged(3)
    remote(VR.at[pl.ds(0, 7)], VR.at[pl.ds(0, 7)], v_s, v_r, (b, r)).wait()
    value = VS[7]
    for j in range(7):
        value = value + VR[j]
    vout[...] = value
    step_y(0).wait_recv()
    step_y(1).wait_recv()
    gout[...] = total + RX[0].astype(F32) + RX[1].astype(F32)

    remote(M.at[pl.ds(0, 31)], N.at[pl.ds(1, 31)], a2a_s, a2a_r, (b, r)).wait_send()
    remote(OWN.at[pl.ds(0, 896), :], OWN.at[pl.ds(0, 896), :], own_s, own_r, (b, r)).wait_send()
    for ch in ("g", "z"):
        buf, _, ss, rs = chans[ch]
        remote(buf.at[pl.ds(0, 15)], buf.at[pl.ds(0, 15)], ss, rs.at[0, 0], (b, r)).wait_send()
    for k in range(4):
        core_swap(k).wait_send()
    for j in (0, 1):
        via(j).wait_send()
        step_y(j).wait_send()


def per_device(features, owner_row, value_probe, grad_probe):
    vmem = pl.BlockSpec(memory_space=pltpu.VMEM)
    dma = pltpu.SemaphoreType.DMA
    return pl.pallas_call(
        kernel,
        out_shape=(jax.ShapeDtypeStruct((8, 128), F32), jax.ShapeDtypeStruct((128, 1024), F32)),
        in_specs=[vmem, vmem, vmem, vmem, pl.BlockSpec(memory_space=pl.ANY)],
        out_specs=(vmem, vmem),
        scratch_shapes=[
            pltpu.VMEM((32, 8, 128), F32),
            pltpu.VMEM((32, 8, 128), F32),
            pltpu.VMEM((16, 128, 1024), BF16),
            pltpu.VMEM((16, 160, 128), BF16),
            pltpu.VMEM((16, 16, 128), F32),
            pltpu.VMEM((1024, 128), BF16),
            pltpu.VMEM((1024, 1), F32),
            pltpu.VMEM((1024, 1024), F32),
            pltpu.VMEM((8, 1024, 128), F32),
            [pltpu.VMEM((512, 512), BF16), pltpu.VMEM((256, 1024), BF16)],
            [pltpu.VMEM((512, 512), F32), pltpu.VMEM((256, 1024), F32)],
            pltpu.VMEM((4, 128, 1024), F32),
            pltpu.VMEM((3, 128, 1024), WIRE),
            pltpu.VMEM((2, 64, 1024), WIRE),
            pltpu.VMEM((2, 128, 1024), WIRE),
            pltpu.VMEM((8, 8, 128), F32),
            pltpu.VMEM((7, 8, 128), F32),
            dma, dma, dma, dma, dma,
            dma, dma((2, 16)),
            dma, dma((2, 16)),
            dma((4,)), dma((4,)), dma((4,)), dma((2,)), dma((2,)), dma, dma,
        ],
        compiler_params=pltpu.CompilerParams(
            collective_id=0, has_side_effects=True, vmem_limit_bytes=56 << 20),
    )(features, owner_row.reshape(1, 128), owner_row.reshape(128, 1), value_probe, grad_probe)


def solution(mesh):
    placed = (P(("blk", "rep"), None), P(("blk", "rep")), P(None, "blk"), P("blk", None))
    return jax.shard_map(
        per_device,
        mesh=mesh,
        in_specs=placed,
        out_specs=(P(None, ("blk", "rep")), P(("blk", "rep"), None)),
        check_vma=False,
    )
```

```python
import functools

import jax
import jax.numpy as jnp
from jax import lax
from jax.experimental import pallas as pl
from jax.experimental.pallas import tpu as pltpu
from jax.sharding import PartitionSpec as P

F32, BF16 = jnp.float32, jnp.bfloat16
MESH = pl.DeviceIdType.MESH
LOG2E = 1.4426950408889634
WIRE = BF16

SLOTS = (
    (0, 0), (1, 0), (3, 0), (0, 1), (0, 3), (1, 1), (3, 1), (3, 3),
    (1, 3), (2, 0), (0, 2), (3, 2), (2, 3), (2, 1), (1, 2), (2, 2),
)
STAGES = {
    "dealt": ((0, 1, 0), (0, 3, 0)),
    "placed": ((0, 0, 1), (0, 0, 3), (1, 0, 1), (1, 0, 3), (1, 1, 0), (1, 3, 0)),
    "t0": ((0, 1, 1), (0, 1, 3), (0, 2, 0), (0, 3, 1), (0, 3, 3), (1, 0), (3, 0), (0, 1)),
    "t0m": ((0, 3), (1, 1), (1, 3), (3, 1), (3, 3), (1, 0, 2), (1, 1, 3)),
    "t1": ((0, 0, 2), (1, 2, 0), (1, 1, 1), (1, 3, 3)),
    "t1m": ((0, 1, 2), (0, 2, 3), (2, 1), (2, 3), (2, 0)),
    "t2": ((1, 3, 1), (0, 2), (3, 2), (0, 3, 2), (1, 2, 3)),
    "t2m": ((0, 2, 1), (1, 2, 1), (1, 3, 2), (1, 2)),
    "last": ((0, 2, 2), (1, 1, 2), (2, 2), (1, 2, 2)),
}
Z_FIRST = ((1, 0), (3, 0), (0, 1), (0, 3), (1, 1), (1, 3), (3, 1), (3, 3))
Z_ON = {
    (1, 0): (((2, 0), 1, 0),),
    (3, 1): (((2, 1), -1, 0),),
    (1, 1): (((1, 2), 0, 1),),
    (3, 3): (((2, 3), -1, 0), ((3, 2), 0, -1)),
    (0, 1): (((0, 2), 0, 1),),
    (2, 1): (((2, 2), 0, 1),),
}


def nt(a, b):
    return lax.dot_general(a, b, (((1,), (1,)), ((), ())), preferred_element_type=F32)


def nn(a, b):
    return jnp.dot(a, b, preferred_element_type=F32)


def split3(a):
    hi = a.astype(BF16)
    rest = a - hi.astype(F32)
    mid = rest.astype(BF16)
    return hi, mid, (rest - mid.astype(F32)).astype(BF16)


def kernel(
    feat, row_r, vprobe, gprobe, vout, gout,
    M, A1, G, Z, W, OWN, BI, X, V, KB, KS, DB, PB, VIA, RX, VT, VS, VR,
    word, st_s, st_r, own_s, own_r, loc, g_s, g_r, z_s, z_r, d_s, d_r, y_s, via_r, rx_r, v_s, v_r,
):
    rho = 512.0 ** -0.25
    c1 = rho * rho * LOG2E
    b, r = lax.axis_index("blk"), lax.axis_index("rep")
    x, z = b % 4, b // 8
    y, core = (b // 4) % 2 * 2 + r // 2, r % 2

    xz = {(dx, dz): ((z + dz) % 4 * 8 + b // 4 % 2 * 4 + (x + dx) % 4, r) for dx in range(4) for dz in range(4) if (dx, dz) != (0, 0)}

    def at_xz(dx, dz):
        return xz[dx % 4, dz % 4]

    ys = [(y + dy) % 4 for dy in range(4)]
    yc = {(dy, dc): (z * 8 + ys[dy] // 2 * 4 + x, ys[dy] % 2 * 2 + (core + dc) % 2) for dy in range(4) for dc in range(2) if (dy, dc) != (0, 0)}

    def at_y(dy, dc):
        return yc[dy % 4, dc]

    def remote(src, dst, ss, rs, dev):
        return pltpu.make_async_remote_copy(
            src_ref=src, dst_ref=dst, send_sem=ss, recv_sem=rs, device_id=dev, device_id_type=MESH)

    mine = pltpu.make_async_copy(gprobe.at[pl.ds(pl.multiple_of(r * 128, 128), 128), :], G.at[0], loc)
    mine.start()

    barrier = pltpu.get_barrier_semaphore()

    def at_half(j):
        return (z * 8 + (y // 2 + j // 4) % 2 * 4 + (x + j) % 4, r)

    peers = [at_half(j) for j in range(1, 8)] + [at_xz(0, d) for d in (1, 2, 3)]
    peers += [at_y(dy, dc) for dy, dc in ((1, 0), (3, 0), (0, 1), (1, 1), (2, 1), (3, 1))]
    for dev in peers:
        pl.semaphore_signal(barrier, inc=1, device_id=dev, device_id_type=MESH)

    orow = jnp.broadcast_to(row_r[...], (128, 128))
    oc = orow.T
    rank = jnp.sum((oc < orow).astype(F32), axis=0, keepdims=True)
    q = lax.broadcasted_iota(jnp.int32, (256, 128), 0)
    pick = (rank == (q // 8 * 4 + q % 4).astype(F32)).astype(BF16)
    slot = (oc % 128).astype(F32).astype(BF16)
    both = nn(pick, jnp.concatenate([feat[...], slot], axis=1))
    M[...] = jnp.where(q % 8 < 4, both[:, :128], both[:, 128:]).reshape(32, 8, 128)
    X[...] = jnp.zeros_like(X)
    V[...] = jnp.zeros_like(V)
    pl.semaphore_wait(barrier, 16)

    for d in (1, 3, 2):
        pl.semaphore_signal(word, inc=1, device_id=at_xz(0, d), device_id_type=MESH)

    def deal(k, _):
        to = (b + k) % 32
        remote(M.at[to], A1.at[k], st_s, st_r, (to, r)).start()
        return 0

    def dealt():
        return remote(A1.at[pl.ds(1, 31)], A1.at[pl.ds(1, 31)], st_s, st_r, (b, r))

    def piece(h, s):
        return G.at[s, pl.ds(h * 64, 64), :]

    def slot_of(h, i1, i2):
        return SLOTS.index((i1 % 4, i2 % 4) if h == 0 else (i2 % 4, i1 % 4))

    def pass_g(h, i1, i2):
        if (i1, i2) != (0, 0):
            s = slot_of(h, i1, i2)
            remote(piece(h, s), piece(h, s), g_s, g_r.at[h, s], (b, r)).wait_recv()
        ways = []
        if i2 == 0:
            ways += [(1, 0)] * (i1 == 0 or (i1 == 1 and h == 0))
            ways += [(-1, 0)] * (i1 == 0 or (i1 == 3 and h == 1))
            ways += [(0, 1), (0, -1)]
        ways += [(0, 1)] * (i2 == 1 and i1 in (0, 1)) + [(0, -1)] * (i2 == 3 and i1 in (3, 2))
        for e1, e2 in ways:
            t = slot_of(h, i1 + e1, i2 + e2)
            remote(piece(h, slot_of(h, i1, i2)), piece(h, t), g_s, g_r.at[h, t],
                   at_xz(e1, e2) if h == 0 else at_xz(e2, e1)).start()

    def send_z(at, to, dx, dz):
        s, t = SLOTS.index(at), SLOTS.index(to)
        remote(Z.at[s], Z.at[t], z_s, z_r.at[t], at_xz(dx, dz)).start()

    def pass_z(dx, dz):
        s = SLOTS.index((dx, dz))
        remote(Z.at[s], Z.at[s], z_s, z_r.at[s], (b, r)).wait_recv()
        for way in Z_ON.get((dx, dz), ()):
            send_z((dx, dz), *way)

    def stage(name):
        for item in STAGES[name]:
            if len(item) == 3:
                pass_g(*item)
            else:
                pass_z(*item)

    mine.wait()
    pass_g(0, 0, 0)
    pl.semaphore_wait(word, 3)
    lax.fori_loop(1, 32, deal, 0)
    A1[0] = M[b]
    pass_g(1, 0, 0)
    stage("dealt")
    dealt().wait_recv()

    n2 = A1[...].reshape(256, 128)
    marks = n2.T[0:1, :]
    lane = lax.broadcasted_iota(jnp.int32, (128, 256), 1)
    want = lax.broadcasted_iota(jnp.int32, (128, 256), 0).astype(F32)
    put = ((marks == want) & (lane % 8 >= 4)).astype(BF16)
    placed32 = nn(put, pltpu.roll(n2, 4, 0).astype(BF16))
    placed = placed32.astype(BF16)
    Z[0, 0:128, :] = placed
    OWN[896:1024, :] = placed
    homes = {
        2: ((0, 128, 0),),
        1: ((64, 64, 256), (0, 64, 512)),
        3: ((0, 64, 320), (64, 64, 576)),
        0: ((0, 128, 768),),
    }
    for dy in (2, 1, 3, 0):
        for dc in (1, 0):
            if (dy, dc) != (0, 0):
                for row, count, at in homes[(-dy) % 4]:
                    remote(OWN.at[pl.ds(896 + row, count), :], OWN.at[pl.ds(at + 128 * (1 - dc), count), :],
                           own_s, own_r, at_y(dy, dc)).start()

    rows = []
    for p in range(8):
        rows.append(jnp.sum((placed32 * G[0, :, p * 128:(p + 1) * 128].astype(F32)).T, axis=0, keepdims=True))
    anchor = jnp.concatenate(rows, axis=0)
    vp = vprobe[:, pl.ds(pl.multiple_of(r * 128, 128), 128)].astype(F32)
    w = vp * (1.0 / rho) - anchor
    norm = (0.5 * c1) * jnp.sum((placed32 * placed32).T, axis=0, keepdims=True)
    eight = lax.broadcasted_iota(jnp.int32, (8, 128), 0)
    n_hi, n_mid, n_lo = split3(jnp.broadcast_to(norm, (8, 128)))
    tail = jnp.where(eight == 0, n_hi.astype(F32), jnp.where(
        eight == 1, n_mid.astype(F32), jnp.where(eight == 2, n_lo.astype(F32), 0.0)))
    Z[0, 128:160, :] = jnp.concatenate([part.astype(F32) for part in split3(w)] + [tail], axis=0).astype(BF16)
    for dx, dz in Z_FIRST:
        send_z((0, 0), (dx, dz), dx, dz)
    stage("placed")

    def unpack(*slots):
        for s in slots:
            aux = Z[s, 128:160, :].astype(F32)
            W[s, 0:8, :] = aux[0:8] + aux[8:16] + aux[16:24]
            W[s, 8:9, :] = aux[24:25] + aux[25:26] + aux[26:27]

    remote(OWN.at[pl.ds(0, 896), :], OWN.at[pl.ds(0, 896), :], own_s, own_r, (b, r)).wait_recv()
    wide = OWN[...].astype(F32)
    BI[...] = (0.5 * c1) * jnp.sum(wide * wide, axis=1, keepdims=True)

    def tile(ii, s0, ns, TI, hook=None):
        TJ = ns * 128
        zz = Z[pl.ds(s0, ns), 0:128, :].reshape(TJ, 128)
        own = OWN[ii, :]
        bj = jnp.concatenate([W[s0 + q, 8:9, :] for q in range(ns)], axis=1)
        k = jnp.exp2(nt(own, zz) * c1 - BI[ii, :] - bj)
        kbig, klow = (KS[0], KB[0]) if TI == 768 else (KS[1], KB[1]) if ns == 8 else (KS[2], KB[2])
        kbig[...] = k * rho
        klow[...] = k.astype(BF16)
        for hh in range(4):
            if hook is not None and hh == 2:
                hook()
            hs = pl.ds(hh * 256, 256)
            X[ii, hs] += nn(klow[...], G[pl.ds(s0, ns), :, hs].reshape(TJ, 256))
            for p in (2 * hh, 2 * hh + 1):
                ps = pl.ds(p * 128, 128)
                inner = nt(own, G[pl.ds(s0, ns), :, ps].reshape(TJ, 128))
                wr = jnp.concatenate([W[s0 + q, p:p + 1, :] for q in range(ns)], axis=1)
                coef = kbig[...] * (inner + wr)
                part = coef[:, 0:128]
                for q in range(1, ns):
                    part = part + coef[:, q * 128:(q + 1) * 128]
                V[p, ii, :] += part
                X[ii, ps] += nn(coef.astype(BF16), zz) * rho

    def early(n, _):
        for m in range(3):
            @pl.when(n == m)
            def _():
                stage("t%d" % m)
                unpack(*range(4 * m, 4 * m + 4))

        def hook():
            for m in range(3):
                @pl.when(n == m)
                def _():
                    stage("t%dm" % m)

        tile(pl.ds(0, 768), n * 4, 4, 768, hook)
        return 0

    lax.fori_loop(0, 3, early, 0)
    stage("last")
    unpack(12, 13, 14, 15)

    def core_swap(k):
        return remote(X.at[pl.ds(pl.multiple_of(k * 256, 256), 128), :], DB.at[k], d_s.at[k], d_r.at[k], at_y(0, 1))

    def merged(k):
        core_swap(k).wait_recv()
        return X[k * 256 + 128:k * 256 + 256, :] + DB[k]

    def via(j):
        half = pl.ds(64 * j, 64)
        return remote(PB.at[0, half, :], VIA.at[j], y_s.at[j], via_r.at[j], at_y(1 - 2 * j, 0))

    def step_y(m, j):
        half = pl.ds(64 * j, 64)
        return remote(PB.at[1 + m, half, :], RX.at[j, pl.ds(64 * ((1 - j) if m == 0 else j), 64), :],
                      y_s.at[2 + 2 * m + j], rx_r.at[2 * m + j], at_y(1 - 2 * j, 0))

    ways = ((2, 1), (2, 0), (1, 1), (1, 0), (3, 1), (3, 0), (0, 1))

    def send_value(i):
        remote(VS.at[i], VR.at[i], v_s, v_r, at_y(*ways[i])).start()

    def finish(k):
        at = pl.multiple_of(k * 256, 256)
        ii = pl.ds(at, 256)
        own = OWN[ii, :].astype(F32) * rho
        lanes = lax.broadcasted_iota(jnp.int32, (256, 128), 1)
        vt = jnp.zeros((256, 128), F32)
        for p in range(8):
            col = jnp.sum(V[p, ii, :], axis=1, keepdims=True)
            X[ii, pl.ds(p * 128, 128)] -= own * col
            vt = jnp.where(lanes == p, col, vt)
        core_swap(k).start()
        VT[2 * k] = vt[0:128].T[0:8]
        VT[2 * k + 1] = vt[128:256].T[0:8]

    def late(k, _):
        tile(pl.ds(pl.multiple_of(k * 256, 256), 256), 12, 4, 256)
        finish(k)

        @pl.when(k == 0)
        def _():
            for c in (0, 1):
                VS[c] = VT[c]
                send_value(c)

        @pl.when(k == 1)
        def _():
            PB[0] = merged(0).astype(WIRE)
            via(0).start()
            via(1).start()

        @pl.when(k == 2)
        def _():
            PB[1] = merged(1).astype(WIRE)
            step_y(0, 0).start()
            step_y(0, 1).start()
            low = lax.broadcasted_iota(jnp.int32, (8, 128), 1) < 64
            for c in (0, 1):
                turned, straight = pltpu.roll(VT[2 + c], 64, 1), VT[4 + c]
                VS[2 + c] = jnp.where(low, straight, turned)
                VS[4 + c] = jnp.where(low, turned, straight)
                send_value(2 + c)
                send_value(4 + c)

        return 0

    lax.fori_loop(0, 3, late, 0)

    def home(n, _):
        tile(pl.ds(768, 256), n * 8, 8, 256)

        @pl.when(n == 0)
        def _():
            whole = merged(2)
            for j in (0, 1):
                via(j).wait_recv()
                PB[2, 64 * j:64 * j + 64, :] = (whole[64 * j:64 * j + 64] + VIA[j].astype(F32)).astype(WIRE)
                step_y(1, j).start()

        return 0

    lax.fori_loop(0, 2, home, 0)
    finish(3)
    VS[6] = VT[6]
    send_value(6)
    total = merged(3)
    remote(VR.at[pl.ds(0, 7)], VR.at[pl.ds(0, 7)], v_s, v_r, (b, r)).wait()
    value = VT[7]
    for j in range(7):
        value = value + VR[j]
    vout[...] = value
    for j in (0, 1):
        step_y(0, j).wait_recv()
        step_y(1, j).wait_recv()
    gout[...] = total + RX[0].astype(F32) + RX[1].astype(F32)

    dealt().wait_send()
    remote(OWN.at[pl.ds(0, 896), :], OWN.at[pl.ds(0, 896), :], own_s, own_r, (b, r)).wait_send()
    remote(G.at[pl.ds(0, 15)], G.at[pl.ds(0, 15)], g_s, g_r.at[0, 0], (b, r)).wait_send()
    remote(Z.at[pl.ds(0, 15)], Z.at[pl.ds(0, 15)], z_s, z_r.at[0], (b, r)).wait_send()
    for k in range(4):
        core_swap(k).wait_send()
    for j in (0, 1):
        via(j).wait_send()
        step_y(0, j).wait_send()
        step_y(1, j).wait_send()


def handed_on(value, grad, vout, gout):
    vout[...] = value[...]
    gout[...] = grad[...]


def per_device(features, owner_row, value_probe, grad_probe):
    vmem = pl.BlockSpec(memory_space=pltpu.VMEM)
    dma = pltpu.SemaphoreType.DMA
    value, grad = pl.pallas_call(
        kernel,
        out_shape=(jax.ShapeDtypeStruct((8, 128), F32), jax.ShapeDtypeStruct((128, 1024), F32)),
        in_specs=[vmem, vmem, vmem, pl.BlockSpec(memory_space=pl.ANY)],
        out_specs=(vmem, vmem),
        scratch_shapes=[
            pltpu.VMEM((32, 8, 128), F32),
            pltpu.VMEM((32, 8, 128), F32),
            pltpu.VMEM((16, 128, 1024), BF16),
            pltpu.VMEM((16, 160, 128), BF16),
            pltpu.VMEM((16, 16, 128), F32),
            pltpu.VMEM((1024, 128), BF16),
            pltpu.VMEM((1024, 1), F32),
            pltpu.VMEM((1024, 1024), F32),
            pltpu.VMEM((8, 1024, 128), F32),
            [pltpu.VMEM((768, 512), BF16), pltpu.VMEM((256, 1024), BF16), pltpu.VMEM((256, 512), BF16)],
            [pltpu.VMEM((768, 512), F32), pltpu.VMEM((256, 1024), F32), pltpu.VMEM((256, 512), F32)],
            pltpu.VMEM((4, 128, 1024), F32),
            pltpu.VMEM((3, 128, 1024), WIRE),
            pltpu.VMEM((2, 64, 1024), WIRE),
            pltpu.VMEM((2, 128, 1024), WIRE),
            pltpu.VMEM((8, 8, 128), F32),
            pltpu.VMEM((7, 8, 128), F32),
            pltpu.VMEM((7, 8, 128), F32),
            pltpu.SemaphoreType.REGULAR, dma, dma, dma, dma, dma,
            dma, dma((2, 16)),
            dma, dma((16,)),
            dma((4,)), dma((4,)), dma((6,)), dma((2,)), dma((4,)), dma, dma,
        ],
        compiler_params=pltpu.CompilerParams(
            collective_id=0, has_side_effects=True, vmem_limit_bytes=56 << 20),
    )(features, owner_row.reshape(1, 128), value_probe, grad_probe)
    return pl.pallas_call(
        handed_on,
        out_shape=(jax.ShapeDtypeStruct((8, 128), F32), jax.ShapeDtypeStruct((128, 1024), F32)),
        in_specs=[vmem, vmem],
        out_specs=(vmem, vmem),
    )(value, grad)


def solution(mesh):
    placed = (P(("blk", "rep"), None), P(("blk", "rep")), P(None, "blk"), P("blk", None))
    return jax.shard_map(
        per_device,
        mesh=mesh,
        in_specs=placed,
        out_specs=(P(None, ("blk", "rep")), P(("blk", "rep"), None)),
        check_vma=False,
    )
```

```python
import functools

import jax
import jax.numpy as jnp
from jax import lax
from jax.experimental import pallas as pl
from jax.experimental.pallas import tpu as pltpu
from jax.sharding import PartitionSpec as P

F32, BF16 = jnp.float32, jnp.bfloat16
MESH = pl.DeviceIdType.MESH
LOG2E = 1.4426950408889634
WIRE = BF16

SLOTS = (
    (0, 0), (3, 0), (0, 3), (1, 0), (0, 1), (1, 3), (3, 3), (1, 1),
    (1, 2), (3, 1), (0, 2), (2, 3), (2, 1), (3, 2), (2, 0), (2, 2),
)
STAGES = {
    "start": ((2, 0, 0, 1, 0), (2, 0, 0, -1, 0)),
    "dealt": ((2, 0, 0, 0, 1), (2, 0, 0, 0, -1), (0, 3, 0), (2, 3, 0, 0, -1), (0, 1, 0), (2, 1, 0, 0, 1)),
    "placed": ((2, 1, 0, 1, 0), (2, 3, 0, -1, 0), (0, 0, 1), (2, 0, 1, 0, 1), (2, 1, 0, 0, -1)),
    "t0": ((1, 3, 1), (3, 3, 1, -1, 0), (0, 1, 1), (2, 1, 1, 0, 1), (2, 3, 0, 0, 1), (1, 3, 0), (1, 0, 3), (0, 0, 3), (1, 1, 0)),
    "t0m": ((1, 3, 3), (3, 3, 3, -1, 0), (1, 1, 1), (3, 1, 1, 0, 1), (3, 0, 3, 0, -1), (0, 2, 0), (2, 2, 0, 0, -1)),
    "t1": ((2, 2, 0, 0, 1), (0, 3, 3), (2, 3, 3, 0, -1), (1, 0, 1), (1, 1, 3), (0, 1, 3)),
    "t1m": ((3, 1, 0, 1, 0), (3, 3, 3, 0, -1)),
    "t2": ((1, 2, 1), (3, 2, 1, 0, 1), (0, 2, 3), (2, 2, 3, 0, -1), (1, 1, 2), (0, 1, 2), (0, 3, 1), (1, 0, 2), (0, 0, 2), (1, 2, 3)),
    "t2m": (),
    "last": ((0, 2, 1), (1, 3, 2), (0, 3, 2), (1, 2, 0), (1, 2, 2), (0, 2, 2)),
}
Z_FIRST = ((1, 0), (3, 0), (0, 1), (0, 3), (1, 1), (3, 1), (1, 3), (3, 3))


def nt(a, b):
    return lax.dot_general(a, b, (((1,), (1,)), ((), ())), preferred_element_type=F32)


def nn(a, b):
    return jnp.dot(a, b, preferred_element_type=F32)


def split3(a):
    hi = a.astype(BF16)
    rest = a - hi.astype(F32)
    mid = rest.astype(BF16)
    return hi, mid, (rest - mid.astype(F32)).astype(BF16)


def kernel(
    feat, row_r, vprobe, gprobe, vout, gout,
    M, A1, G, Z, W, OWN, BI, X, V, KB, KS, DB, PB, VIA, RX, VT, VS, VR,
    word, st_s, st_r, own_s, own_r, loc, g_s, g_r, z_s, z_r, d_s, d_r, y_s, via_r, rx_r, v_s, v_r,
):
    rho = 512.0 ** -0.25
    c1 = rho * rho * LOG2E
    b, r = lax.axis_index("blk"), lax.axis_index("rep")
    x, z = b % 4, b // 8
    y, core = (b // 4) % 2 * 2 + r // 2, r % 2

    xz = {(dx, dz): ((z + dz) % 4 * 8 + b // 4 % 2 * 4 + (x + dx) % 4, r) for dx in range(4) for dz in range(4) if (dx, dz) != (0, 0)}

    def at_xz(dx, dz):
        return xz[dx % 4, dz % 4]

    uv = {}
    for du, dv in xz:
        (b0, _), (b1, _) = xz[du, dv], xz[dv, du]
        uv[du, dv] = (b0 + core * (b1 - b0), r)

    def at_uv(du, dv):
        return uv[du % 4, dv % 4]

    ys = [(y + dy) % 4 for dy in range(4)]
    yc = {(dy, dc): (z * 8 + ys[dy] // 2 * 4 + x, ys[dy] % 2 * 2 + (core + dc) % 2) for dy in range(4) for dc in range(2) if (dy, dc) != (0, 0)}

    def at_y(dy, dc):
        return yc[dy % 4, dc]

    def remote(src, dst, ss, rs, dev):
        return pltpu.make_async_remote_copy(
            src_ref=src, dst_ref=dst, send_sem=ss, recv_sem=rs, device_id=dev, device_id_type=MESH)

    mine = pltpu.make_async_copy(gprobe.at[pl.ds(pl.multiple_of(r * 128, 128), 128), :], G.at[0], loc)
    mine.start()

    barrier = pltpu.get_barrier_semaphore()

    def at_half(j):
        return (z * 8 + (y // 2 + j // 4) % 2 * 4 + (x + j) % 4, r)

    peers = [at_half(j) for j in range(1, 8)] + [at_xz(0, d) for d in (1, 2, 3)]
    peers += [at_y(dy, dc) for dy, dc in ((1, 0), (3, 0), (0, 1), (1, 1), (2, 1), (3, 1))]
    for dev in peers:
        pl.semaphore_signal(barrier, inc=1, device_id=dev, device_id_type=MESH)

    orow = jnp.broadcast_to(row_r[...], (128, 128))
    oc = orow.T
    rank = jnp.sum((oc < orow).astype(F32), axis=0, keepdims=True)
    q = lax.broadcasted_iota(jnp.int32, (256, 128), 0)
    pick = (rank == (q // 8 * 4 + q % 4).astype(F32)).astype(BF16)
    slot = (oc % 128).astype(F32).astype(BF16)
    both = nn(pick, jnp.concatenate([feat[...], slot], axis=1))
    M[...] = jnp.where(q % 8 < 4, both[:, :128], both[:, 128:]).reshape(32, 8, 128)
    X[...] = jnp.zeros_like(X)
    V[...] = jnp.zeros_like(V)
    pl.semaphore_wait(barrier, 16)

    for d in (1, 3, 2):
        pl.semaphore_signal(word, inc=1, device_id=at_xz(0, d), device_id_type=MESH)

    def deal(k, _):
        to = (b + k) % 32
        remote(M.at[to], A1.at[k], st_s, st_r, (to, r)).start()
        return 0

    def dealt():
        return remote(A1.at[pl.ds(1, 31)], A1.at[pl.ds(1, 31)], st_s, st_r, (b, r))

    def do(kind, du, dv, eu=0, ev=0):
        buf, ss, rs = (G, g_s, g_r) if kind % 2 == 0 else (Z, z_s, z_r)
        s, t = SLOTS.index((du, dv)), SLOTS.index(((du + eu) % 4, (dv + ev) % 4))
        if kind == 2 and ev == 0 and du != 0:
            half = pl.ds(0 if eu == 1 else 64, 64)
            remote(buf.at[s, half, :], buf.at[t, half, :], ss, rs.at[t], at_uv(eu, ev)).start()
        elif kind < 2:
            remote(buf.at[s], buf.at[s], ss, rs.at[s], (b, r)).wait_recv()
        else:
            remote(buf.at[s], buf.at[t], ss, rs.at[t], at_uv(eu, ev)).start()

    def stage(name):
        for item in STAGES[name]:
            do(*item)

    mine.wait()
    stage("start")
    pl.semaphore_wait(word, 3)
    lax.fori_loop(1, 32, deal, 0)
    A1[0] = M[b]
    stage("dealt")
    dealt().wait_recv()

    n2 = A1[...].reshape(256, 128)
    marks = n2.T[0:1, :]
    lane = lax.broadcasted_iota(jnp.int32, (128, 256), 1)
    want = lax.broadcasted_iota(jnp.int32, (128, 256), 0).astype(F32)
    put = ((marks == want) & (lane % 8 >= 4)).astype(BF16)
    placed32 = nn(put, pltpu.roll(n2, 4, 0).astype(BF16))
    placed = placed32.astype(BF16)
    Z[0, 0:128, :] = placed
    OWN[896:1024, :] = placed
    homes = {
        2: ((0, 128, 0),),
        1: ((64, 64, 256), (0, 64, 512)),
        3: ((0, 64, 320), (64, 64, 576)),
        0: ((0, 128, 768),),
    }
    for dy in (2, 1, 3, 0):
        for dc in (1, 0):
            if (dy, dc) != (0, 0):
                for row, count, at in homes[(-dy) % 4]:
                    remote(OWN.at[pl.ds(896 + row, count), :], OWN.at[pl.ds(at + 128 * (1 - dc), count), :],
                           own_s, own_r, at_y(dy, dc)).start()

    rows = []
    for p in range(8):
        rows.append(jnp.sum((placed32 * G[0, :, p * 128:(p + 1) * 128].astype(F32)).T, axis=0, keepdims=True))
    anchor = jnp.concatenate(rows, axis=0)
    vp = vprobe[:, pl.ds(pl.multiple_of(r * 128, 128), 128)].astype(F32)
    w = vp * (1.0 / rho) - anchor
    norm = (0.5 * c1) * jnp.sum((placed32 * placed32).T, axis=0, keepdims=True)
    eight = lax.broadcasted_iota(jnp.int32, (8, 128), 0)
    n_hi, n_mid, n_lo = split3(jnp.broadcast_to(norm, (8, 128)))
    tail = jnp.where(eight == 0, n_hi.astype(F32), jnp.where(
        eight == 1, n_mid.astype(F32), jnp.where(eight == 2, n_lo.astype(F32), 0.0)))
    Z[0, 128:160, :] = jnp.concatenate([part.astype(F32) for part in split3(w)] + [tail], axis=0).astype(BF16)
    for dx, dz in Z_FIRST:
        do(3, 0, 0, dx, dz)
    stage("placed")

    def unpack(*slots):
        for s in slots:
            aux = Z[s, 128:160, :].astype(F32)
            W[s, 0:8, :] = aux[0:8] + aux[8:16] + aux[16:24]
            W[s, 8:9, :] = aux[24:25] + aux[25:26] + aux[26:27]

    remote(OWN.at[pl.ds(0, 896), :], OWN.at[pl.ds(0, 896), :], own_s, own_r, (b, r)).wait_recv()
    wide = OWN[...].astype(F32)
    BI[...] = (0.5 * c1) * jnp.sum(wide * wide, axis=1, keepdims=True)

    def tile(ii, s0, ns, TI, hook=None):
        TJ = ns * 128
        zz = Z[pl.ds(s0, ns), 0:128, :].reshape(TJ, 128)
        own = OWN[ii, :]
        bj = jnp.concatenate([W[s0 + q, 8:9, :] for q in range(ns)], axis=1)
        k = jnp.exp2(nt(own, zz) * c1 - BI[ii, :] - bj)
        kbig, klow = (KS[0], KB[0]) if TI == 768 else (KS[1], KB[1]) if ns == 8 else (KS[2], KB[2])
        kbig[...] = k * rho
        klow[...] = k.astype(BF16)
        for hh in range(4):
            if hook is not None and hh == 2:
                hook()
            hs = pl.ds(hh * 256, 256)
            X[ii, hs] += nn(klow[...], G[pl.ds(s0, ns), :, hs].reshape(TJ, 256))
            for p in (2 * hh, 2 * hh + 1):
                ps = pl.ds(p * 128, 128)
                inner = nt(own, G[pl.ds(s0, ns), :, ps].reshape(TJ, 128))
                wr = jnp.concatenate([W[s0 + q, p:p + 1, :] for q in range(ns)], axis=1)
                coef = kbig[...] * (inner + wr)
                part = coef[:, 0:128]
                for q in range(1, ns):
                    part = part + coef[:, q * 128:(q + 1) * 128]
                V[p, ii, :] += part
                X[ii, ps] += nn(coef.astype(BF16), zz) * rho

    def early(n, _):
        for m in range(3):
            @pl.when(n == m)
            def _():
                stage("t%d" % m)
                unpack(*range(4 * m, 4 * m + 4))

        def hook():
            for m in range(3):
                @pl.when(n == m)
                def _():
                    stage("t%dm" % m)

        tile(pl.ds(0, 768), n * 4, 4, 768, hook)
        return 0

    lax.fori_loop(0, 3, early, 0)
    stage("last")
    unpack(12, 13, 14, 15)

    def core_swap(k):
        return remote(X.at[pl.ds(pl.multiple_of(k * 256, 256), 128), :], DB.at[k], d_s.at[k], d_r.at[k], at_y(0, 1))

    def merged(k):
        core_swap(k).wait_recv()
        return X[k * 256 + 128:k * 256 + 256, :] + DB[k]

    def via(j):
        half = pl.ds(64 * j, 64)
        return remote(PB.at[0, half, :], VIA.at[j], y_s.at[j], via_r.at[j], at_y(1 - 2 * j, 0))

    def step_y(m, j):
        half = pl.ds(64 * j, 64)
        return remote(PB.at[1 + m, half, :], RX.at[j, pl.ds(64 * ((1 - j) if m == 0 else j), 64), :],
                      y_s.at[2 + 2 * m + j], rx_r.at[2 * m + j], at_y(1 - 2 * j, 0))

    ways = ((2, 1), (2, 0), (1, 1), (1, 0), (3, 1), (3, 0), (0, 1))

    def send_value(i):
        remote(VS.at[i], VR.at[i], v_s, v_r, at_y(*ways[i])).start()

    def finish(k):
        at = pl.multiple_of(k * 256, 256)
        ii = pl.ds(at, 256)
        own = OWN[ii, :].astype(F32) * rho
        lanes = lax.broadcasted_iota(jnp.int32, (256, 128), 1)
        vt = jnp.zeros((256, 128), F32)
        for p in range(8):
            col = jnp.sum(V[p, ii, :], axis=1, keepdims=True)
            X[ii, pl.ds(p * 128, 128)] -= own * col
            vt = jnp.where(lanes == p, col, vt)
        core_swap(k).start()
        VT[2 * k] = vt[0:128].T[0:8]
        VT[2 * k + 1] = vt[128:256].T[0:8]

    def late(k, _):
        def hook():
            @pl.when(k == 1)
            def _():
                PB[0] = merged(0).astype(WIRE)
                via(0).start()
                via(1).start()

            @pl.when(k == 2)
            def _():
                PB[1] = merged(1).astype(WIRE)
                step_y(0, 0).start()
                step_y(0, 1).start()

        tile(pl.ds(pl.multiple_of(k * 256, 256), 256), 12, 4, 256, hook)
        finish(k)

        @pl.when(k == 0)
        def _():
            for c in (0, 1):
                VS[c] = VT[c]
                send_value(c)

        @pl.when(k == 2)
        def _():
            low = lax.broadcasted_iota(jnp.int32, (8, 128), 1) < 64
            for c in (0, 1):
                turned, straight = pltpu.roll(VT[2 + c], 64, 1), VT[4 + c]
                VS[2 + c] = jnp.where(low, straight, turned)
                VS[4 + c] = jnp.where(low, turned, straight)
                send_value(2 + c)
                send_value(4 + c)

        return 0

    lax.fori_loop(0, 3, late, 0)

    def joined():
        whole = merged(2)
        for j in (0, 1):
            via(j).wait_recv()
            PB[2, 64 * j:64 * j + 64, :] = (whole[64 * j:64 * j + 64] + VIA[j].astype(F32)).astype(WIRE)
            step_y(1, j).start()

    def home(n, _):
        def hook():
            @pl.when(n == 0)
            def _():
                joined()

        tile(pl.ds(768, 256), n * 8, 8, 256, hook)
        return 0

    lax.fori_loop(0, 2, home, 0)
    finish(3)
    VS[6] = VT[6]
    send_value(6)
    total = merged(3)
    remote(VR.at[pl.ds(0, 7)], VR.at[pl.ds(0, 7)], v_s, v_r, (b, r)).wait()
    value = VT[7]
    for j in range(7):
        value = value + VR[j]
    vout[...] = value
    for j in (0, 1):
        step_y(0, j).wait_recv()
        step_y(1, j).wait_recv()
    gout[...] = total + RX[0].astype(F32) + RX[1].astype(F32)

    dealt().wait_send()
    remote(OWN.at[pl.ds(0, 896), :], OWN.at[pl.ds(0, 896), :], own_s, own_r, (b, r)).wait_send()
    remote(G.at[pl.ds(0, 15)], G.at[pl.ds(0, 15)], g_s, g_r.at[0], (b, r)).wait_send()
    remote(Z.at[pl.ds(0, 15)], Z.at[pl.ds(0, 15)], z_s, z_r.at[0], (b, r)).wait_send()
    for k in range(4):
        core_swap(k).wait_send()
    for j in (0, 1):
        via(j).wait_send()
        step_y(0, j).wait_send()
        step_y(1, j).wait_send()


def handed_on(value, grad, vout, gout):
    vout[...] = value[...]
    gout[...] = grad[...]


def per_device(features, owner_row, value_probe, grad_probe):
    vmem = pl.BlockSpec(memory_space=pltpu.VMEM)
    dma = pltpu.SemaphoreType.DMA
    value, grad = pl.pallas_call(
        kernel,
        out_shape=(jax.ShapeDtypeStruct((8, 128), F32), jax.ShapeDtypeStruct((128, 1024), F32)),
        in_specs=[vmem, vmem, vmem, pl.BlockSpec(memory_space=pl.ANY)],
        out_specs=(vmem, vmem),
        scratch_shapes=[
            pltpu.VMEM((32, 8, 128), F32),
            pltpu.VMEM((32, 8, 128), F32),
            pltpu.VMEM((16, 128, 1024), BF16),
            pltpu.VMEM((16, 160, 128), BF16),
            pltpu.VMEM((16, 16, 128), F32),
            pltpu.VMEM((1024, 128), BF16),
            pltpu.VMEM((1024, 1), F32),
            pltpu.VMEM((1024, 1024), F32),
            pltpu.VMEM((8, 1024, 128), F32),
            [pltpu.VMEM((768, 512), BF16), pltpu.VMEM((256, 1024), BF16), pltpu.VMEM((256, 512), BF16)],
            [pltpu.VMEM((768, 512), F32), pltpu.VMEM((256, 1024), F32), pltpu.VMEM((256, 512), F32)],
            pltpu.VMEM((4, 128, 1024), F32),
            pltpu.VMEM((3, 128, 1024), WIRE),
            pltpu.VMEM((2, 64, 1024), WIRE),
            pltpu.VMEM((2, 128, 1024), WIRE),
            pltpu.VMEM((8, 8, 128), F32),
            pltpu.VMEM((7, 8, 128), F32),
            pltpu.VMEM((7, 8, 128), F32),
            pltpu.SemaphoreType.REGULAR, dma, dma, dma, dma, dma,
            dma, dma((16,)),
            dma, dma((16,)),
            dma((4,)), dma((4,)), dma((6,)), dma((2,)), dma((4,)), dma, dma,
        ],
        compiler_params=pltpu.CompilerParams(
            collective_id=0, has_side_effects=True, vmem_limit_bytes=56 << 20),
    )(features, owner_row.reshape(1, 128), value_probe, grad_probe)
    return pl.pallas_call(
        handed_on,
        out_shape=(jax.ShapeDtypeStruct((8, 128), F32), jax.ShapeDtypeStruct((128, 1024), F32)),
        in_specs=[vmem, vmem],
        out_specs=(vmem, vmem),
    )(value, grad)


def solution(mesh):
    placed = (P(("blk", "rep"), None), P(("blk", "rep")), P(None, "blk"), P("blk", None))
    return jax.shard_map(
        per_device,
        mesh=mesh,
        in_specs=placed,
        out_specs=(P(None, ("blk", "rep")), P(("blk", "rep"), None)),
        check_vma=False,
    )
```
